32 devices in a mesh: blk: 4 (over y, core), seq: 8 (over z, x).
Axes of the slice: x: 2, y: 2, z: 4, core: 2. Of those that a mesh axis runs over, the one named last changes fastest.
Arguments:
- scores: bfloat16 [512, 43008], P('seq', 'blk'), may hold values from 0.09 to 136
- counts: int32 [512], P('seq'), may hold values from 1 to 64
Outputs:
- covariance_tiles: float32 [4, 10752, 43008], P(None, 'seq', 'blk')
The draws below stay inside these ranges and needn't reach their ends.
All inputs are finite; a program needn't handle non-finite values.
Results may differ from the reference program's by a relative error of at most 0.0023.
Values may be sent and summed in bfloat16 or wider, within the bound.
No kernel may reach another device: no remote copies, remote signals or barrier semaphores. Data moves between devices by JAX's collectives and lax.ppermute only.
A program may use at most 320 MiB of HBM per device.

```python
import jax
import jax.numpy as jnp
from jax import lax

STATES = 21
POSITIONS = 2048
SEQS = 512
BLOCK_COLS = 10752
ROUNDS = 3
N_BLK = 4


def draw_scores(key, part):
    key = jax.random.fold_in(key, 11)
    key_label, key_motif, key_keep, key_noise, key_soft = jax.random.split(key, 5)
    labels = jax.random.randint(key_label, (SEQS,), 0, 6)
    motifs = jax.random.randint(key_motif, (6, POSITIONS), 0, STATES)
    keeping = jax.random.randint(key_keep, (SEQS, POSITIONS), 0, 10) < 6
    noise = jax.random.randint(key_noise, (SEQS, POSITIONS), 0, STATES)
    chosen = motifs[labels]
    hard = jnp.where(keeping, chosen, noise).astype(jnp.int32)
    hits = (hard[:, :, None] == jnp.arange(STATES, dtype=jnp.int32)).astype(jnp.float32)
    rough = jax.random.normal(key_soft, (SEQS, POSITIONS, STATES), jnp.float32)
    rough = jnp.clip(rough, -3.0, 3.0)
    values = jnp.exp(2.5 * hits + 0.8 * rough)
    return values.reshape(SEQS, POSITIONS * STATES).astype(jnp.bfloat16)


def draw_counts(key, part):
    key = jax.random.fold_in(key, 12)
    rows_index = jnp.arange(SEQS, dtype=jnp.int32)
    ceiling = 2 + rows_index * 62 // SEQS
    drawn = 1 + jax.random.randint(key, (SEQS,), 0, ceiling)
    drawn = jnp.where(rows_index == SEQS - 1, 64, drawn)
    drawn = jnp.where(rows_index == 0, 1, drawn)
    return drawn.astype(jnp.int32)


def setup_inputs(seed: int = 0) -> dict:
    key_of = jax.random.split(jax.random.key(seed), 3)
    scores = draw_scores(jax.random.fold_in(key_of[2], 71), 0)
    counts = draw_counts(jax.random.fold_in(key_of[2], 71), 0)
    return dict(scores=scores, counts=counts)


def reference(scores, counts):
    raw = scores.astype(jnp.float32).reshape(SEQS, POSITIONS, STATES)
    profile = raw / lax.optimization_barrier(jnp.sum(raw, axis=2, keepdims=True))
    profile = profile.reshape(SEQS, POSITIONS * STATES)
    weight = 1.0 / counts.astype(jnp.float32)
    total = jnp.sum(weight)
    freq = lax.optimization_barrier(jnp.sum(weight[:, None] * profile, axis=0)) / total
    scaled = jnp.sqrt(weight * STATES / total)
    centered = (scaled[:, None] * (profile - freq[None, :])).astype(jnp.bfloat16)
    blocks = centered.reshape(SEQS, N_BLK, BLOCK_COLS)
    result = jnp.zeros((ROUNDS + 1, BLOCK_COLS, POSITIONS * STATES), jnp.float32)

    def fill(block_id, result):
        block_id = jnp.asarray(block_id).astype(jnp.int32)
        mine_cols = lax.dynamic_index_in_dim(blocks, block_id, 1, keepdims=False)
        for shift_by in range(ROUNDS + 1):
            partner = jnp.mod(block_id - shift_by + N_BLK, N_BLK).astype(jnp.int32)
            other_cols = lax.dynamic_index_in_dim(blocks, partner, 1, keepdims=False)
            tile = jnp.dot(other_cols.T, mine_cols, preferred_element_type=jnp.float32)
            result = lax.dynamic_update_slice(result, tile[None].astype(result.dtype), (jnp.int32(shift_by), jnp.int32(0), (block_id * BLOCK_COLS).astype(jnp.int32)))
        return result
    return lax.fori_loop(0, N_BLK, fill, result)
```

```python
import functools

import jax
import jax.numpy as jnp
from jax import lax
from jax.experimental import pallas as pl
from jax.experimental.pallas import tpu as pltpu
from jax.sharding import PartitionSpec as P

STATES = 21
LANE = 128
VMEM_LIMIT = 56 * 2**20


def from_behind(value, axis, steps):
    count = lax.axis_size(axis)
    pairs = [(source, (source + steps) % count) for source in range(count)]
    return lax.ppermute(value, axis, pairs)


def partner_stripes(stripe_here):
    rounds_count = min(4, lax.axis_size("blk") - 1)
    received = [stripe_here]
    for shift_by in range(1, rounds_count + 1):
        received.append(from_behind(stripe_here, "blk", shift_by))
    return jnp.stack(received, axis=0)


def plain_body(scores, counts):
    seq_rows = scores.shape[0]
    block_pos = scores.shape[1] // STATES
    raw = scores.astype(jnp.float32).reshape(seq_rows, block_pos, STATES)
    profile = raw / jnp.sum(raw, axis=2, keepdims=True)
    profile = profile.reshape(seq_rows, block_pos * STATES)
    weight = 1.0 / counts.astype(jnp.float32)
    total_weight, frequency = lax.psum(
        (jnp.sum(weight), jnp.sum(weight[:, None] * profile, axis=0)), "seq"
    )
    freq = frequency / total_weight
    scaled = jnp.sqrt(weight * STATES / total_weight)
    centered = (scaled[:, None] * (profile - freq[None, :])).astype(jnp.bfloat16)
    block_cols = centered.shape[1]
    stripe_width = block_cols // lax.axis_size("seq")
    gathered = lax.all_gather(centered, "seq", axis=0, tiled=True)
    seq_index = lax.axis_index("seq")
    stripe_here = lax.dynamic_slice_in_dim(gathered, seq_index * stripe_width, stripe_width, 1)
    partners = partner_stripes(stripe_here)
    return jnp.einsum("kmr,mc->krc", partners, gathered, preferred_element_type=jnp.float32)


def center_kernel(raw_ref, weight_ref, out_ref):
    seqs, width = raw_ref.shape
    pos = width // STATES
    raw = raw_ref[...]
    first = STATES * lax.broadcasted_iota(jnp.int32, (pos, width), 0)
    here = lax.broadcasted_iota(jnp.int32, (pos, width), 1)
    member = ((here >= first) & (here < first + STATES)).astype(jnp.bfloat16)
    sums = lax.dot_general(
        raw, member, (((1,), (1,)), ((), ())), preferred_element_type=jnp.float32
    )
    high = sums.astype(jnp.bfloat16)
    rest = sums - high.astype(jnp.float32)
    mid = rest.astype(jnp.bfloat16)
    low = (rest - mid.astype(jnp.float32)).astype(jnp.bfloat16)
    spread = (
        jnp.dot(high, member, preferred_element_type=jnp.float32)
        + jnp.dot(mid, member, preferred_element_type=jnp.float32)
    ) + jnp.dot(low, member, preferred_element_type=jnp.float32)
    profile = raw.astype(jnp.float32) / spread
    weight = weight_ref[...]
    total = jnp.sum(weight, axis=0, keepdims=True)
    freq = jnp.sum(weight * profile, axis=0, keepdims=True) / total
    scaled = jnp.sqrt(weight * STATES / total)
    centered = (scaled * (profile - freq)).astype(jnp.bfloat16)
    out_ref[...] = centered.T


def center(raw, weight):
    seqs, width = raw.shape
    vmem = pl.BlockSpec(memory_space=pltpu.VMEM)
    return pl.pallas_call(
        center_kernel,
        out_shape=jax.ShapeDtypeStruct((width, seqs), jnp.bfloat16),
        in_specs=[vmem, vmem],
        out_specs=vmem,
        compiler_params=pltpu.CompilerParams(vmem_limit_bytes=VMEM_LIMIT),
        name="center",
    )(raw, weight.reshape(seqs, 1))


def tiles_kernel(lefts, sizes, tall, split, where, *refs):
    left, refs = refs[:lefts], refs[lefts:]
    pieces, refs = refs[: len(sizes)], refs[len(sizes) :]
    out, left_buf, right, out_buf, left_sem, right_sem, out_sem = refs[-7:]
    stripe = left[0].shape[0]
    width = right.shape[0]
    per = stripe // tall
    steps = lefts * per
    small = tall // split
    column = pl.multiple_of(where[0] * LANE, LANE)
    rounds = 1 + 2 * len(sizes)

    def load(step, act):
        which = step // per
        row = pl.multiple_of(lax.rem(step, per) * tall, 16)
        slot = lax.rem(step, 2)
        for j in range(lefts):

            @pl.when(which == j)
            def _():
                act(pltpu.make_async_copy(
                    left[j].at[pl.ds(row, tall)], left_buf.at[slot], left_sem.at[slot]
                ))

    def store(step, j):
        row = pl.multiple_of(lax.rem(step, per) * tall, 8)
        slot = lax.rem(step, 2)
        return pltpu.make_async_copy(
            out_buf.at[slot, pl.ds(j * small, small)],
            out.at[where[rounds + step // per], pl.ds(row + j * small, small), pl.ds(column, width)],
            out_sem.at[slot, j],
        )

    gather = [
        pltpu.make_async_copy(
            pieces[i].at[pl.ds(pl.multiple_of(where[1 + 2 * i], 16), size)],
            right.at[pl.ds(pl.multiple_of(where[2 + 2 * i], 16), size)],
            right_sem.at[i],
        )
        for i, size in enumerate(sizes)
    ]
    load(0, lambda copy: copy.start())
    for copy in gather:
        copy.start()
    for copy in gather:
        copy.wait()

    def body(step, _):
        slot = lax.rem(step, 2)

        @pl.when(step + 1 < steps)
        def _():
            load(step + 1, lambda copy: copy.start())

        load(step, lambda copy: copy.wait())
        for j in range(split):

            @pl.when(step >= 2)
            def _():
                store(step - 2, j).wait()

            out_buf[slot, j * small : (j + 1) * small, :] = lax.dot_general(
                left_buf[slot, j * small : (j + 1) * small, :],
                right[...],
                (((1,), (1,)), ((), ())),
                preferred_element_type=jnp.float32,
            )
            store(step, j).start()
        return 0

    lax.fori_loop(0, steps, body, 0)
    for step in (steps - 2, steps - 1):
        for j in range(split):
            store(step, j).wait()


def tiles(out, out_shape, column, left, rounds, pieces, width, tall=672, split=2):
    stripe, depth = left[0].shape
    sizes = tuple(size for _, _, size, _ in pieces)
    where = [column]
    for _, source, _, target in pieces:
        where += [source, target]
    where = jnp.stack([jnp.asarray(v, jnp.int32) for v in where + list(rounds)])
    anywhere = pl.BlockSpec(memory_space=pl.ANY)
    operands = [where, *left, *(piece[0] for piece in pieces)]
    specs = [pl.BlockSpec(memory_space=pltpu.SMEM)] + [anywhere] * (len(operands) - 1)
    aliases = {}
    if out is not None:
        aliases = {len(operands): 0}
        operands.append(out)
        specs.append(anywhere)
    return pl.pallas_call(
        functools.partial(tiles_kernel, len(left), sizes, tall, split),
        out_shape=jax.ShapeDtypeStruct(out_shape, jnp.float32),
        in_specs=specs,
        out_specs=anywhere,
        scratch_shapes=[
            pltpu.VMEM((2, tall, depth), jnp.bfloat16),
            pltpu.VMEM((width, depth), jnp.bfloat16),
            pltpu.VMEM((2, tall, width), jnp.float32),
            pltpu.SemaphoreType.DMA((2,)),
            pltpu.SemaphoreType.DMA((len(sizes),)),
            pltpu.SemaphoreType.DMA((2, split)),
        ],
        input_output_aliases=aliases,
        compiler_params=pltpu.CompilerParams(vmem_limit_bytes=VMEM_LIMIT),
        cost_estimate=pl.CostEstimate(
            flops=2 * len(left) * stripe * width * depth,
            bytes_accessed=4 * len(left) * stripe * width,
            transcendentals=0,
        ),
        name="tiles",
    )(*operands)


def flip(value, axis, bits):
    count = lax.axis_size(axis)
    return lax.ppermute(value, axis, [(source, source ^ bits) for source in range(count)])


def wait_all(*values):
    return lax.optimization_barrier(values)


def fast_body(scores, counts):
    blocks, seqs_axis = lax.axis_size("blk"), lax.axis_size("seq")
    stripe = scores.shape[1] // seqs_axis
    out_shape = (blocks, stripe, scores.shape[1])
    raw = lax.all_to_all(scores, "seq", 1, 0, tiled=True)
    all_counts = lax.all_gather(counts, "seq", axis=0, tiled=True)
    weight = 1.0 / all_counts.astype(jnp.float32)
    own = center(raw, weight)

    seq, blk = lax.axis_index("seq"), lax.axis_index("blk")
    x, z, core = seq % 2, seq // 2, blk % 2
    middle = (z == 1) | (z == 2)
    rounds = [0, 2, 3 - 2 * core, 1 + 2 * core]
    pair_tiles = 2 * stripe // LANE

    def pair(out, flipped, mine, others, left, rounds):
        pieces = [(mine, 0, stripe, x * stripe)]
        row = (1 - x) * stripe
        for other in others:
            pieces.append((other, 0, other.shape[0], row))
            row = row + other.shape[0]
        column = (z ^ flipped) * pair_tiles
        return tiles(out, out_shape, column, left, rounds, pieces, 2 * stripe)

    x_own = flip(own, "seq", 1)
    z1 = flip(own, "seq", 2)
    z3_middle = lax.ppermute(own, "seq", [(2, 4), (4, 2), (3, 5), (5, 3)])
    y_own = flip(own, "blk", 2)
    core_own = flip(own, "blk", 1)
    own, x_own, z1, z3_middle, y_own, core_own = wait_all(
        own, x_own, z1, z3_middle, y_own, core_own
    )
    core_y = flip(y_own, "blk", 1)
    x_z1 = flip(z1, "seq", 1)
    z3_outer = lax.ppermute(own, "seq", [(0, 6), (6, 0), (1, 7), (7, 1)])
    left = [own, y_own, core_own, core_y]
    out = pair(None, 0, own, [x_own], left, rounds)
    out, x_z1, z3_outer = wait_all(out, x_z1, z3_outer)
    z3 = jnp.where(middle, z3_middle, z3_outer)
    x_z3 = flip(z3, "seq", 1)
    z2 = flip(z3, "seq", 2)
    out = pair(out, 1, z1, [x_z1], left, rounds)
    out, x_z3, z2 = wait_all(out, x_z3, z2)
    half = stripe // 2
    x_z2 = [flip(z2[:half], "seq", 1), flip(x_z3[half:], "seq", 2)]
    out = pair(out, 3, z3, [x_z3], left, rounds)
    out = pair(out, 2, z2, x_z2, left, rounds)
    return out


def solution(mesh):
    def body(scores, counts):
        stripe_width = scores.shape[1] // mesh.shape["seq"]
        fits = (
            mesh.shape["blk"] == 4
            and mesh.shape["seq"] == 8
            and stripe_width % 64 == 0
            and stripe_width % STATES == 0
            and stripe_width % 672 == 0
        )
        return (fast_body if fits else plain_body)(scores, counts)

    return jax.shard_map(
        body,
        mesh=mesh,
        in_specs=(P("seq", "blk"), P("seq")),
        out_specs=P(None, "seq", "blk"),
        check_vma=False,
    )
```

```python
import functools

import jax
import jax.numpy as jnp
from jax import lax
from jax.experimental import pallas as pl
from jax.experimental.pallas import tpu as pltpu
from jax.sharding import PartitionSpec as P

STATES = 21
LANE = 128
LOCAL_VMEM = 36 * 2**20
SPARE_VMEM = 10 * 2**20


def from_behind(value, axis, steps):
    count = lax.axis_size(axis)
    pairs = [(source, (source + steps) % count) for source in range(count)]
    return lax.ppermute(value, axis, pairs)


def partner_stripes(stripe_here):
    rounds_count = min(4, lax.axis_size("blk") - 1)
    received = [stripe_here]
    for shift_by in range(1, rounds_count + 1):
        received.append(from_behind(stripe_here, "blk", shift_by))
    return jnp.stack(received, axis=0)


def plain_body(scores, counts):
    seq_rows = scores.shape[0]
    block_pos = scores.shape[1] // STATES
    raw = scores.astype(jnp.float32).reshape(seq_rows, block_pos, STATES)
    profile = raw / jnp.sum(raw, axis=2, keepdims=True)
    profile = profile.reshape(seq_rows, block_pos * STATES)
    weight = 1.0 / counts.astype(jnp.float32)
    total_weight, frequency = lax.psum(
        (jnp.sum(weight), jnp.sum(weight[:, None] * profile, axis=0)), "seq"
    )
    freq = frequency / total_weight
    scaled = jnp.sqrt(weight * STATES / total_weight)
    centered = (scaled[:, None] * (profile - freq[None, :])).astype(jnp.bfloat16)
    block_cols = centered.shape[1]
    stripe_width = block_cols // lax.axis_size("seq")
    gathered = lax.all_gather(centered, "seq", axis=0, tiled=True)
    seq_index = lax.axis_index("seq")
    stripe_here = lax.dynamic_slice_in_dim(gathered, seq_index * stripe_width, stripe_width, 1)
    partners = partner_stripes(stripe_here)
    return jnp.einsum("kmr,mc->krc", partners, gathered, preferred_element_type=jnp.float32)


def payload_kernel(scores_ref, counts_ref, out_ref):
    parts, rows, width = out_ref.shape
    stripe = scores_ref.shape[1] // parts
    counts = jnp.broadcast_to(counts_ref[...].astype(jnp.float32), (rows, rows)).T
    tail = counts[:, : width - stripe].astype(jnp.bfloat16)
    for j in range(parts):
        out_ref[j, :, :stripe] = scores_ref[:, j * stripe : (j + 1) * stripe]
        out_ref[j, :, stripe:] = tail


def payload(scores, counts, parts):
    rows, columns = scores.shape
    stripe = columns // parts
    vmem = pl.BlockSpec(memory_space=pltpu.VMEM)
    return pl.pallas_call(
        payload_kernel,
        out_shape=jax.ShapeDtypeStruct((parts, rows, stripe + LANE // 2), jnp.bfloat16),
        in_specs=[vmem, vmem],
        out_specs=vmem,
        compiler_params=pltpu.CompilerParams(vmem_limit_bytes=LOCAL_VMEM),
        name="payload",
    )(scores, counts.reshape(1, rows))


def center_kernel(raw_ref, out_ref):
    width = out_ref.shape[0]
    pos = width // STATES
    raw = raw_ref[:, :width]
    counts = raw_ref[:, width:].astype(jnp.float32)[:, :1]

    def members(copies):
        shape = (copies * pos, width)
        row = lax.broadcasted_iota(jnp.int32, shape, 0)
        for _ in range(copies - 1):
            row = jnp.where(row >= pos, row - pos, row)
        first = STATES * row
        here = lax.broadcasted_iota(jnp.int32, shape, 1)
        return ((here >= first) & (here < first + STATES)).astype(jnp.bfloat16)

    sums = lax.dot_general(
        raw, members(1), (((1,), (1,)), ((), ())), preferred_element_type=jnp.float32
    )
    high = sums.astype(jnp.bfloat16)
    rest = sums - high.astype(jnp.float32)
    mid = rest.astype(jnp.bfloat16)
    low = (rest - mid.astype(jnp.float32)).astype(jnp.bfloat16)
    terms = jnp.concatenate([high, mid, low], axis=1)
    spread = jnp.dot(terms, members(3), preferred_element_type=jnp.float32)
    profile = raw.astype(jnp.float32) / spread
    weight = 1.0 / counts
    total = jnp.sum(weight, axis=0, keepdims=True)
    freq = jnp.sum(weight * profile, axis=0, keepdims=True) / total
    scaled = jnp.sqrt(weight * STATES / total)
    centered = (scaled * (profile - freq)).astype(jnp.bfloat16)
    out_ref[...] = centered.T


def center(raw, stripe):
    seqs = raw.shape[0]
    vmem = pl.BlockSpec(memory_space=pltpu.VMEM)
    return pl.pallas_call(
        center_kernel,
        out_shape=jax.ShapeDtypeStruct((stripe, seqs), jnp.bfloat16),
        in_specs=[vmem],
        out_specs=vmem,
        compiler_params=pltpu.CompilerParams(vmem_limit_bytes=LOCAL_VMEM),
        name="center",
    )(raw)


FIRST, SECOND, PAIR = "first", "second", "pair"


def width_of(form, stripe):
    whole = stripe // LANE * LANE
    return {FIRST: whole, SECOND: 2 * stripe - whole, PAIR: 2 * stripe}[form]


def fill_right(form, right, mine, other, x):
    stripe = sum(ref.shape[0] for ref in mine)
    width = right.shape[0]
    whole = stripe // LANE * LANE
    cut = stripe - whole

    def rows(ref, start, size):
        return ref[pl.ds(pl.multiple_of(start, 16), size), :]

    def put(refs, row):
        for ref in refs:
            right[pl.ds(pl.multiple_of(row, 16), ref.shape[0]), :] = ref[...]
            row = row + ref.shape[0]

    if form == PAIR:
        put(mine, x * stripe)
        put(other, (1 - x) * stripe)
        return 0
    if form == SECOND:
        put(other, (1 - x) * cut)

        @pl.when(x == 0)
        def _():
            last = mine[-1]
            right[:cut, :] = last[last.shape[0] - cut :, :]

        @pl.when(x != 0)
        def _():
            right[stripe:, :] = mine[0][:cut, :]

        return (1 - x) * ((2 * stripe - width) // LANE)

    @pl.when(x == 0)
    def _():
        row = 0
        for ref in mine:
            size = min(ref.shape[0], width - row)
            right[row : row + size, :] = ref[:size, :]
            row += size

    @pl.when(x != 0)
    def _():
        row, skip = 0, cut
        for ref in mine:
            size = ref.shape[0] - skip
            right[row : row + size, :] = ref[skip:, :]
            row, skip = row + size, 0

    return x * ((2 * stripe - width) // LANE)


def tiles_kernel(jobs, joining, aliased, slots, *refs):
    if joining:
        parts, refs = refs[:joining], refs[joining:]
    else:
        left, refs = refs[0], refs[1:]
    pieces = []
    for _, _, mine, other, _ in jobs:
        pieces.append((refs[:mine], refs[mine : mine + other]))
        refs = refs[mine + other :]
    if aliased:
        refs = refs[1:]
    out, refs = refs[0], refs[1:]
    if joining:
        left, refs = refs[0], refs[1:]
    rights, (out_buf, out_sem) = refs[:-2], refs[-2:]
    seq, core = lax.axis_index("seq"), lax.rem(lax.axis_index("blk"), 2)
    x, z = lax.rem(seq, 2), seq // 2
    tall = out_buf.shape[1]
    stripe = out.shape[1]
    per = stripe // tall
    if joining:
        for j in range(joining):
            left[j * stripe : (j + 1) * stripe, :] = parts[j][...]

    def store(job, tile, step):
        which = step // per
        round_ = jnp.where(
            which == 0, 0, jnp.where(which == 1, 3 - 2 * core, jnp.where(which == 2, 2, 1 + 2 * core))
        )
        width = rights[job].shape[0]
        slot = lax.rem(step, slots)
        row = pl.multiple_of(lax.rem(step, per) * tall, 16)
        return pltpu.make_async_copy(
            out_buf.at[slot, :, pl.ds(0, width)],
            out.at[round_, pl.ds(row, tall), pl.ds(pl.multiple_of(tile * LANE, LANE), width)],
            out_sem.at[slot],
        )

    before = None
    for job, (form, flipped, _, _, (low, high)) in enumerate(jobs):
        low, high = low * per, high * per
        right = rights[job]
        tile = (z ^ flipped) * (2 * stripe // LANE) + fill_right(form, right, *pieces[job], x)
        here = functools.partial(store, job, tile)

        def body(step, _, here=here, before=before, right=right, low=low):
            if before is not None:

                @pl.when(step < low + slots)
                def _():
                    before(step).wait()

            @pl.when(step >= low + slots)
            def _():
                here(step).wait()

            out_buf[lax.rem(step, slots), :, : right.shape[0]] = lax.dot_general(
                left[pl.ds(pl.multiple_of(step * tall, 16), tall), :],
                right[...],
                (((1,), (1,)), ((), ())),
                preferred_element_type=jnp.float32,
            )
            here(step).start()
            return 0

        lax.fori_loop(low, high, body, 0)
        before = here
    for slot in range(slots):
        before(jnp.int32(slot)).wait()


def tiles(out, out_shape, left, jobs, slots=4):
    joining = len(left) if isinstance(left, list) else 0
    stripe = out_shape[1]
    depth = (left[0] if joining else left).shape[1]
    tall = stripe // 4
    widths = [width_of(form, stripe) for form, *_ in jobs]
    vmem = pl.BlockSpec(memory_space=pltpu.VMEM)
    anywhere = pl.BlockSpec(memory_space=pl.ANY)
    operands = list(left) if joining else [left]
    for _, _, mine, other, _ in jobs:
        operands += [*mine, *other]
    specs = [vmem] * len(operands)
    aliases = {}
    if out is not None:
        aliases = {len(operands): 0}
        operands.append(out)
        specs.append(anywhere)
    shapes, out_specs = [jax.ShapeDtypeStruct(out_shape, jnp.float32)], [anywhere]
    if joining:
        shapes.append(jax.ShapeDtypeStruct((joining * stripe, depth), jnp.bfloat16))
        out_specs.append(vmem)
    forms = [(form, pair, len(mine), len(other), part) for form, pair, mine, other, part in jobs]
    scratch = sum(widths) * depth * 2 + slots * tall * max(widths) * 4
    columns = sum(width * (part[1] - part[0]) for width, (*_, part) in zip(widths, jobs))
    result = pl.pallas_call(
        functools.partial(tiles_kernel, forms, joining, out is not None, slots),
        out_shape=shapes,
        in_specs=specs,
        out_specs=out_specs,
        scratch_shapes=[pltpu.VMEM((width, depth), jnp.bfloat16) for width in widths]
        + [
            pltpu.VMEM((slots, tall, max(widths)), jnp.float32),
            pltpu.SemaphoreType.DMA((slots,)),
        ],
        input_output_aliases=aliases,
        compiler_params=pltpu.CompilerParams(vmem_limit_bytes=scratch + SPARE_VMEM),
        cost_estimate=pl.CostEstimate(
            flops=2 * stripe * columns * depth,
            bytes_accessed=4 * stripe * columns,
            transcendentals=0,
        ),
        name="tiles",
    )(*operands)
    return result if joining else result[0]


def flip(value, axis, bits):
    count = lax.axis_size(axis)
    return lax.ppermute(value, axis, [(source, source ^ bits) for source in range(count)])


def wait_all(*values):
    return lax.optimization_barrier(values)


def fast_body(scores, counts):
    blocks, parts = lax.axis_size("blk"), lax.axis_size("seq")
    stripe = scores.shape[1] // parts
    out_shape = (blocks, stripe, scores.shape[1])
    raw = lax.all_to_all(payload(scores, counts, parts), "seq", 0, 0, tiled=True)
    own = center(raw.reshape(-1, raw.shape[-1]), stripe)

    z = lax.axis_index("seq") // 2
    middle = (z == 1) | (z == 2)
    z1 = flip(own, "seq", 2)
    x_own = flip(own, "seq", 1)
    z3_middle = lax.ppermute(own, "seq", [(2, 4), (4, 2), (3, 5), (5, 3)])
    y_own = flip(own, "blk", 2)
    core_own = flip(own, "blk", 1)
    z3_outer = lax.ppermute(own, "seq", [(0, 6), (6, 0), (1, 7), (7, 1)])
    out, _ = tiles(None, out_shape, [own, core_own], [(FIRST, 0, [own], [], (0, 2))])
    own, x_own, z1, z3_middle, y_own, core_own, out = wait_all(
        own, x_own, z1, z3_middle, y_own, core_own, out
    )
    x_z1 = flip(z1, "seq", 1)
    core_y = flip(y_own, "blk", 1)
    every = (0, 4)
    out, left = tiles(
        out,
        out_shape,
        [own, core_own, y_own, core_y],
        [
            (SECOND, 0, [own], [x_own], every),
            (FIRST, 0, [own], [], (2, 4)),
            (FIRST, 1, [z1], [], every),
        ],
    )
    out, x_z1, z3_outer = wait_all(out, x_z1, z3_outer)
    half = stripe // 2
    z3 = [
        jnp.where(middle, z3_middle[rows], z3_outer[rows])
        for rows in (slice(0, half), slice(half, stripe))
    ]
    x_z3_low = flip(z3[1], "seq", 1)
    z2_top = flip(z3[0], "seq", 2)
    x_z3 = [flip(z3[0], "seq", 1), x_z3_low]
    z2 = [z2_top, flip(z3[1], "seq", 2)]
    out = tiles(out, out_shape, left, [(SECOND, 1, [z1], [x_z1], every), (FIRST, 3, z3, [], every)])
    out, z2[0], x_z3[1] = wait_all(out, z2[0], x_z3[1])
    x_z2 = [flip(z2[0], "seq", 1), flip(x_z3[1], "seq", 2)]
    out = tiles(out, out_shape, left, [(SECOND, 3, z3, x_z3, every), (FIRST, 2, z2, [], every)])
    return tiles(out, out_shape, left, [(SECOND, 2, z2, x_z2, every)])


def solution(mesh):
    def body(scores, counts):
        stripe_width = scores.shape[1] // mesh.shape["seq"]
        fits = (
            mesh.shape["blk"] == 4
            and mesh.shape["seq"] == 8
            and stripe_width % 64 == 0
            and stripe_width % STATES == 0
            and stripe_width % 64 == 0
        )
        return (fast_body if fits else plain_body)(scores, counts)

    return jax.shard_map(
        body,
        mesh=mesh,
        in_specs=(P("seq", "blk"), P("seq")),
        out_specs=P(None, "seq", "blk"),
        check_vma=False,
    )
```

```python
import functools

import jax
import jax.numpy as jnp
from jax import lax
from jax.experimental import pallas as pl
from jax.experimental.pallas import tpu as pltpu
from jax.sharding import PartitionSpec as P

STATES = 21
LANE = 128
LOCAL_VMEM = 36 * 2**20
SPARE_VMEM = 10 * 2**20


def from_behind(value, axis, steps):
    count = lax.axis_size(axis)
    pairs = [(source, (source + steps) % count) for source in range(count)]
    return lax.ppermute(value, axis, pairs)


def partner_stripes(stripe_here):
    rounds_count = min(4, lax.axis_size("blk") - 1)
    received = [stripe_here]
    for shift_by in range(1, rounds_count + 1):
        received.append(from_behind(stripe_here, "blk", shift_by))
    return jnp.stack(received, axis=0)


def plain_body(scores, counts):
    seq_rows = scores.shape[0]
    block_pos = scores.shape[1] // STATES
    raw = scores.astype(jnp.float32).reshape(seq_rows, block_pos, STATES)
    profile = raw / jnp.sum(raw, axis=2, keepdims=True)
    profile = profile.reshape(seq_rows, block_pos * STATES)
    weight = 1.0 / counts.astype(jnp.float32)
    total_weight, frequency = lax.psum(
        (jnp.sum(weight), jnp.sum(weight[:, None] * profile, axis=0)), "seq"
    )
    freq = frequency / total_weight
    scaled = jnp.sqrt(weight * STATES / total_weight)
    centered = (scaled[:, None] * (profile - freq[None, :])).astype(jnp.bfloat16)
    block_cols = centered.shape[1]
    stripe_width = block_cols // lax.axis_size("seq")
    gathered = lax.all_gather(centered, "seq", axis=0, tiled=True)
    seq_index = lax.axis_index("seq")
    stripe_here = lax.dynamic_slice_in_dim(gathered, seq_index * stripe_width, stripe_width, 1)
    partners = partner_stripes(stripe_here)
    return jnp.einsum("kmr,mc->krc", partners, gathered, preferred_element_type=jnp.float32)


def payload_kernel(scores_ref, counts_ref, *refs):
    out, cut = refs[:-1], refs[-1]
    parts, rows, width = cut.shape
    stripe = scores_ref.shape[1] // parts
    counts = jnp.broadcast_to(counts_ref[...].astype(jnp.float32), (rows, rows)).T
    tail = counts[:, : width - stripe].astype(jnp.bfloat16)
    for j in range(parts):
        cut[j, :, :stripe] = scores_ref[:, j * stripe : (j + 1) * stripe]
        cut[j, :, stripe:] = tail
    for m in range(parts):
        out[m][...] = cut[lax.axis_index("seq") ^ m]


def payload(scores, counts, parts):
    rows, columns = scores.shape
    width = columns // parts + LANE // 2
    vmem = pl.BlockSpec(memory_space=pltpu.VMEM)
    return pl.pallas_call(
        payload_kernel,
        out_shape=[jax.ShapeDtypeStruct((rows, width), jnp.bfloat16)] * parts,
        in_specs=[vmem, vmem],
        out_specs=[vmem] * parts,
        scratch_shapes=[pltpu.VMEM((parts, rows, width), jnp.bfloat16)],
        compiler_params=pltpu.CompilerParams(vmem_limit_bytes=LOCAL_VMEM),
        name="payload",
    )(scores, counts.reshape(1, rows))


def center_kernel(order, *refs):
    pieces, out_ref, raw_ref = refs[:-2], refs[-2], refs[-1]
    width = out_ref.shape[0]
    for bits, piece in zip(order, pieces):
        rows = piece.shape[0]
        first = pl.multiple_of((lax.axis_index("seq") ^ bits) * rows, 16)
        raw_ref[pl.ds(first, rows), :] = piece[...]
    pos = width // STATES
    raw = raw_ref[:, :width]
    counts = raw_ref[:, width:].astype(jnp.float32)[:, :1]

    def members(copies):
        shape = (copies * pos, width)
        row = lax.broadcasted_iota(jnp.int32, shape, 0)
        for _ in range(copies - 1):
            row = jnp.where(row >= pos, row - pos, row)
        first = STATES * row
        here = lax.broadcasted_iota(jnp.int32, shape, 1)
        return ((here >= first) & (here < first + STATES)).astype(jnp.bfloat16)

    sums = lax.dot_general(
        raw, members(1), (((1,), (1,)), ((), ())), preferred_element_type=jnp.float32
    )
    high = sums.astype(jnp.bfloat16)
    rest = sums - high.astype(jnp.float32)
    mid = rest.astype(jnp.bfloat16)
    low = (rest - mid.astype(jnp.float32)).astype(jnp.bfloat16)
    terms = jnp.concatenate([high, mid, low], axis=1)
    spread = jnp.dot(terms, members(3), preferred_element_type=jnp.float32)
    profile = raw.astype(jnp.float32) / spread
    weight = 1.0 / counts
    total = jnp.sum(weight, axis=0, keepdims=True)
    freq = jnp.sum(weight * profile, axis=0, keepdims=True) / total
    scaled = jnp.sqrt(weight * STATES / total)
    centered = (scaled * (profile - freq)).astype(jnp.bfloat16)
    out_ref[...] = centered.T


def center(order, pieces, stripe):
    rows, width = pieces[0].shape
    seqs = rows * len(pieces)
    vmem = pl.BlockSpec(memory_space=pltpu.VMEM)
    return pl.pallas_call(
        functools.partial(center_kernel, order),
        out_shape=jax.ShapeDtypeStruct((stripe, seqs), jnp.bfloat16),
        in_specs=[vmem] * len(pieces),
        out_specs=vmem,
        scratch_shapes=[pltpu.VMEM((seqs, width), jnp.bfloat16)],
        compiler_params=pltpu.CompilerParams(vmem_limit_bytes=LOCAL_VMEM),
        name="center",
    )(*pieces)


FIRST, SECOND, PAIR = "first", "second", "pair"


def width_of(form, stripe):
    whole = stripe // LANE * LANE
    return {FIRST: whole, SECOND: 2 * stripe - whole, PAIR: 2 * stripe}[form]


def fill_right(form, right, mine, other, x):
    stripe = sum(ref.shape[0] for ref in mine)
    width = right.shape[0]
    whole = stripe // LANE * LANE
    cut = stripe - whole

    def rows(ref, start, size):
        return ref[pl.ds(pl.multiple_of(start, 16), size), :]

    def put(refs, row):
        for ref in refs:
            right[pl.ds(pl.multiple_of(row, 16), ref.shape[0]), :] = ref[...]
            row = row + ref.shape[0]

    if form == PAIR:
        put(mine, x * stripe)
        put(other, (1 - x) * stripe)
        return 0
    if form == SECOND:
        put(other, (1 - x) * cut)

        @pl.when(x == 0)
        def _():
            last = mine[-1]
            right[:cut, :] = last[last.shape[0] - cut :, :]

        @pl.when(x != 0)
        def _():
            right[stripe:, :] = mine[0][:cut, :]

        return (1 - x) * ((2 * stripe - width) // LANE)

    @pl.when(x == 0)
    def _():
        row = 0
        for ref in mine:
            size = min(ref.shape[0], width - row)
            right[row : row + size, :] = ref[:size, :]
            row += size

    @pl.when(x != 0)
    def _():
        row, skip = 0, cut
        for ref in mine:
            size = ref.shape[0] - skip
            right[row : row + size, :] = ref[skip:, :]
            row, skip = row + size, 0

    return x * ((2 * stripe - width) // LANE)


def tiles_kernel(jobs, joining, aliased, slots, *refs):
    if joining:
        parts, refs = refs[:joining], refs[joining:]
    else:
        left, refs = refs[0], refs[1:]
    pieces = []
    for _, _, mine, other, _ in jobs:
        pieces.append((refs[:mine], refs[mine : mine + other]))
        refs = refs[mine + other :]
    if aliased:
        refs = refs[1:]
    out, refs = refs[0], refs[1:]
    if joining:
        left, refs = refs[0], refs[1:]
    rights, (out_buf, out_sem) = refs[:-2], refs[-2:]
    seq, core = lax.axis_index("seq"), lax.rem(lax.axis_index("blk"), 2)
    x, z = lax.rem(seq, 2), seq // 2
    tall = out_buf.shape[1]
    stripe = out.shape[1]
    per = stripe // tall
    if joining:
        for j in range(joining):
            left[j * stripe : (j + 1) * stripe, :] = parts[j][...]

    def store(job, tile, shift, step):
        which = step // per
        round_ = jnp.where(
            which == 0, 0, jnp.where(which == 1, 3 - 2 * core, jnp.where(which == 2, 2, 1 + 2 * core))
        )
        width = rights[job].shape[0]
        slot = lax.rem(step + shift, slots)
        row = pl.multiple_of(lax.rem(step, per) * tall, 16)
        return pltpu.make_async_copy(
            out_buf.at[slot, :, pl.ds(0, width)],
            out.at[round_, pl.ds(row, tall), pl.ds(pl.multiple_of(tile * LANE, LANE), width)],
            out_sem.at[slot],
        )

    before, shift = None, 0
    for job, (form, flipped, _, _, (low, high)) in enumerate(jobs):
        low, high = low * per, high * per
        shift -= low
        right = rights[job]
        tile = (z ^ flipped) * (2 * stripe // LANE) + fill_right(form, right, *pieces[job], x)
        here = functools.partial(store, job, tile, shift % slots)

        def body(step, _, here=here, before=before, right=right, low=low, shift=shift % slots):
            if before is not None:

                @pl.when(step < low + slots)
                def _():
                    before(step - low).wait()

            @pl.when(step >= low + slots)
            def _():
                here(step).wait()

            out_buf[lax.rem(step + shift, slots), :, : right.shape[0]] = lax.dot_general(
                left[pl.ds(pl.multiple_of(step * tall, 16), tall), :],
                right[...],
                (((1,), (1,)), ((), ())),
                preferred_element_type=jnp.float32,
            )
            here(step).start()
            return 0

        lax.fori_loop(low, high, body, 0)
        shift += high
        before = functools.partial(store, job, tile, shift % slots)
    for step in range(slots):
        before(jnp.int32(step)).wait()


def tiles(out, out_shape, left, jobs, slots=3):
    joining = len(left) if isinstance(left, list) else 0
    stripe = out_shape[1]
    depth = (left[0] if joining else left).shape[1]
    tall = stripe // 2
    widths = [width_of(form, stripe) for form, *_ in jobs]
    vmem = pl.BlockSpec(memory_space=pltpu.VMEM)
    anywhere = pl.BlockSpec(memory_space=pl.ANY)
    operands = list(left) if joining else [left]
    for _, _, mine, other, _ in jobs:
        operands += [*mine, *other]
    specs = [vmem] * len(operands)
    aliases = {}
    if out is not None:
        aliases = {len(operands): 0}
        operands.append(out)
        specs.append(anywhere)
    shapes, out_specs = [jax.ShapeDtypeStruct(out_shape, jnp.float32)], [anywhere]
    if joining:
        shapes.append(jax.ShapeDtypeStruct((joining * stripe, depth), jnp.bfloat16))
        out_specs.append(vmem)
    forms = [(form, pair, len(mine), len(other), part) for form, pair, mine, other, part in jobs]
    scratch = sum(widths) * depth * 2 + slots * tall * max(widths) * 4
    columns = sum(width * (part[1] - part[0]) for width, (*_, part) in zip(widths, jobs))
    result = pl.pallas_call(
        functools.partial(tiles_kernel, forms, joining, out is not None, slots),
        out_shape=shapes,
        in_specs=specs,
        out_specs=out_specs,
        scratch_shapes=[pltpu.VMEM((width, depth), jnp.bfloat16) for width in widths]
        + [
            pltpu.VMEM((slots, tall, max(widths)), jnp.float32),
            pltpu.SemaphoreType.DMA((slots,)),
        ],
        input_output_aliases=aliases,
        compiler_params=pltpu.CompilerParams(vmem_limit_bytes=scratch + SPARE_VMEM),
        cost_estimate=pl.CostEstimate(
            flops=2 * stripe * columns * depth,
            bytes_accessed=4 * stripe * columns,
            transcendentals=0,
        ),
        name="tiles",
    )(*operands)
    return result if joining else result[0]


def flip(value, axis, bits):
    count = lax.axis_size(axis)
    return lax.ppermute(value, axis, [(source, source ^ bits) for source in range(count)])


def wait_all(*values):
    return lax.optimization_barrier(values)


def fast_body(scores, counts):
    blocks, parts = lax.axis_size("blk"), lax.axis_size("seq")
    stripe = scores.shape[1] // parts
    out_shape = (blocks, stripe, scores.shape[1])
    pieces = payload(scores, counts, parts)
    order = (6, 7, 4, 5, 2, 3, 1, 0)
    own = center(
        order,
        [flip(pieces[bits], "seq", bits) if bits else pieces[0] for bits in order],
        stripe,
    )

    z = lax.axis_index("seq") // 2
    middle = (z == 1) | (z == 2)
    z1 = flip(own, "seq", 2)
    x_own = flip(own, "seq", 1)
    z3_middle = lax.ppermute(own, "seq", [(2, 4), (4, 2), (3, 5), (5, 3)])
    y_own = flip(own, "blk", 2)
    core_own = flip(own, "blk", 1)
    z3_outer = lax.ppermute(own, "seq", [(0, 6), (6, 0), (1, 7), (7, 1)])
    out, _ = tiles(None, out_shape, [own, core_own], [(FIRST, 0, [own], [], (0, 2))])
    x_own, z1, z3_middle, y_own, out = wait_all(x_own, z1, z3_middle, y_own, out)
    x_z1 = flip(z1, "seq", 1)
    core_y = flip(y_own, "blk", 1)
    every = (0, 4)
    out, left = tiles(
        out,
        out_shape,
        [own, core_own, y_own, core_y],
        [
            (SECOND, 0, [own], [x_own], every),
            (FIRST, 0, [own], [], (2, 4)),
            (FIRST, 1, [z1], [], every),
        ],
    )
    out, x_z1, z3_outer = wait_all(out, x_z1, z3_outer)
    half = stripe // 2
    z3 = [
        jnp.where(middle, z3_middle[rows], z3_outer[rows])
        for rows in (slice(0, half), slice(half, stripe))
    ]
    x_z3_low = flip(z3[1], "seq", 1)
    z2_top = flip(z3[0], "seq", 2)
    x_z3 = [flip(z3[0], "seq", 1), x_z3_low]
    z2 = [z2_top, flip(z3[1], "seq", 2)]
    out = tiles(out, out_shape, left, [(SECOND, 1, [z1], [x_z1], every), (FIRST, 3, z3, [], every)])
    out, z2[0], x_z3[1] = wait_all(out, z2[0], x_z3[1])
    x_z2 = [flip(z2[0], "seq", 1), flip(x_z3[1], "seq", 2)]
    out = tiles(out, out_shape, left, [(SECOND, 3, z3, x_z3, every), (FIRST, 2, z2, [], every)])
    return tiles(out, out_shape, left, [(SECOND, 2, z2, x_z2, every)])


def solution(mesh):
    def body(scores, counts):
        stripe_width = scores.shape[1] // mesh.shape["seq"]
        fits = (
            mesh.shape["blk"] == 4
            and mesh.shape["seq"] == 8
            and stripe_width % 64 == 0
            and stripe_width % STATES == 0
            and stripe_width % 64 == 0
        )
        return (fast_body if fits else plain_body)(scores, counts)

    return jax.shard_map(
        body,
        mesh=mesh,
        in_specs=(P("seq", "blk"), P("seq")),
        out_specs=P(None, "seq", "blk"),
        check_vma=False,
    )
```

```python
import functools

import jax
import jax.numpy as jnp
from jax import lax
from jax.experimental import pallas as pl
from jax.experimental.pallas import tpu as pltpu
from jax.sharding import PartitionSpec as P

STATES = 21
LANE = 128
LOCAL_VMEM = 36 * 2**20
SPARE_VMEM = 10 * 2**20


def from_behind(value, axis, steps):
    count = lax.axis_size(axis)
    pairs = [(source, (source + steps) % count) for source in range(count)]
    return lax.ppermute(value, axis, pairs)


def partner_stripes(stripe_here):
    rounds_count = min(4, lax.axis_size("blk") - 1)
    received = [stripe_here]
    for shift_by in range(1, rounds_count + 1):
        received.append(from_behind(stripe_here, "blk", shift_by))
    return jnp.stack(received, axis=0)


def plain_body(scores, counts):
    seq_rows = scores.shape[0]
    block_pos = scores.shape[1] // STATES
    raw = scores.astype(jnp.float32).reshape(seq_rows, block_pos, STATES)
    profile = raw / jnp.sum(raw, axis=2, keepdims=True)
    profile = profile.reshape(seq_rows, block_pos * STATES)
    weight = 1.0 / counts.astype(jnp.float32)
    total_weight, frequency = lax.psum(
        (jnp.sum(weight), jnp.sum(weight[:, None] * profile, axis=0)), "seq"
    )
    freq = frequency / total_weight
    scaled = jnp.sqrt(weight * STATES / total_weight)
    centered = (scaled[:, None] * (profile - freq[None, :])).astype(jnp.bfloat16)
    block_cols = centered.shape[1]
    stripe_width = block_cols // lax.axis_size("seq")
    gathered = lax.all_gather(centered, "seq", axis=0, tiled=True)
    seq_index = lax.axis_index("seq")
    stripe_here = lax.dynamic_slice_in_dim(gathered, seq_index * stripe_width, stripe_width, 1)
    partners = partner_stripes(stripe_here)
    return jnp.einsum("kmr,mc->krc", partners, gathered, preferred_element_type=jnp.float32)


def payload_kernel(scores_ref, counts_ref, *refs):
    out, cut = refs[:-1], refs[-1]
    parts, rows, width = cut.shape
    stripe = scores_ref.shape[1] // parts
    counts = jnp.broadcast_to(counts_ref[...].astype(jnp.float32), (rows, rows)).T
    tail = counts[:, : width - stripe].astype(jnp.bfloat16)
    for j in range(parts):
        cut[j, :, :stripe] = scores_ref[:, j * stripe : (j + 1) * stripe]
        cut[j, :, stripe:] = tail
    for m in range(parts):
        out[m][...] = cut[lax.axis_index("seq") ^ m]


def payload(scores, counts, parts):
    rows, columns = scores.shape
    width = columns // parts + LANE // 2
    vmem = pl.BlockSpec(memory_space=pltpu.VMEM)
    return pl.pallas_call(
        payload_kernel,
        out_shape=[jax.ShapeDtypeStruct((rows, width), jnp.bfloat16)] * parts,
        in_specs=[vmem, vmem],
        out_specs=[vmem] * parts,
        scratch_shapes=[pltpu.VMEM((parts, rows, width), jnp.bfloat16)],
        compiler_params=pltpu.CompilerParams(vmem_limit_bytes=LOCAL_VMEM),
        name="payload",
    )(scores, counts.reshape(1, rows))


def center_kernel(order, *refs):
    pieces, out_ref, raw_ref = refs[:-2], refs[-2], refs[-1]
    width = out_ref.shape[0]
    for bits, piece in zip(order, pieces):
        rows = piece.shape[0]
        first = pl.multiple_of((lax.axis_index("seq") ^ bits) * rows, 16)
        raw_ref[pl.ds(first, rows), :] = piece[...]
    pos = width // STATES
    raw = raw_ref[:, :width]
    counts = raw_ref[:, width:].astype(jnp.float32)[:, :1]

    def members(copies):
        shape = (copies * pos, width)
        row = lax.broadcasted_iota(jnp.int32, shape, 0)
        for _ in range(copies - 1):
            row = jnp.where(row >= pos, row - pos, row)
        first = STATES * row
        here = lax.broadcasted_iota(jnp.int32, shape, 1)
        return ((here >= first) & (here < first + STATES)).astype(jnp.bfloat16)

    sums = lax.dot_general(
        raw, members(1), (((1,), (1,)), ((), ())), preferred_element_type=jnp.float32
    )
    high = sums.astype(jnp.bfloat16)
    rest = sums - high.astype(jnp.float32)
    mid = rest.astype(jnp.bfloat16)
    low = (rest - mid.astype(jnp.float32)).astype(jnp.bfloat16)
    terms = jnp.concatenate([high, mid, low], axis=1)
    spread = jnp.dot(terms, members(3), preferred_element_type=jnp.float32)
    profile = raw.astype(jnp.float32) / spread
    weight = 1.0 / counts
    total = jnp.sum(weight, axis=0, keepdims=True)
    freq = jnp.sum(weight * profile, axis=0, keepdims=True) / total
    scaled = jnp.sqrt(weight * STATES / total)
    centered = (scaled * (profile - freq)).astype(jnp.bfloat16)
    out_ref[...] = centered.T


def center(order, pieces, stripe):
    rows, width = pieces[0].shape
    seqs = rows * len(pieces)
    vmem = pl.BlockSpec(memory_space=pltpu.VMEM)
    return pl.pallas_call(
        functools.partial(center_kernel, order),
        out_shape=jax.ShapeDtypeStruct((stripe, seqs), jnp.bfloat16),
        in_specs=[vmem] * len(pieces),
        out_specs=vmem,
        scratch_shapes=[pltpu.VMEM((seqs, width), jnp.bfloat16)],
        compiler_params=pltpu.CompilerParams(vmem_limit_bytes=LOCAL_VMEM),
        name="center",
    )(*pieces)


FIRST, SECOND, PAIR = "first", "second", "pair"


def width_of(form, stripe):
    whole = stripe // LANE * LANE
    return {FIRST: whole, SECOND: 2 * stripe - whole, PAIR: 2 * stripe}[form]


def fill_right(form, right, mine, other, x):
    stripe = sum(ref.shape[0] for ref in mine)
    width = right.shape[0]
    whole = stripe // LANE * LANE
    cut = stripe - whole

    def rows(ref, start, size):
        return ref[pl.ds(pl.multiple_of(start, 16), size), :]

    def put(refs, row):
        for ref in refs:
            right[pl.ds(pl.multiple_of(row, 16), ref.shape[0]), :] = ref[...]
            row = row + ref.shape[0]

    if form == PAIR:
        put(mine, x * stripe)
        put(other, (1 - x) * stripe)
        return 0
    if form == SECOND:
        put(other, (1 - x) * cut)

        @pl.when(x == 0)
        def _():
            last = mine[-1]
            right[:cut, :] = last[last.shape[0] - cut :, :]

        @pl.when(x != 0)
        def _():
            right[stripe:, :] = mine[0][:cut, :]

        return (1 - x) * ((2 * stripe - width) // LANE)

    @pl.when(x == 0)
    def _():
        row = 0
        for ref in mine:
            size = min(ref.shape[0], width - row)
            right[row : row + size, :] = ref[:size, :]
            row += size

    @pl.when(x != 0)
    def _():
        row, skip = 0, cut
        for ref in mine:
            size = ref.shape[0] - skip
            right[row : row + size, :] = ref[skip:, :]
            row, skip = row + size, 0

    return x * ((2 * stripe - width) // LANE)


def tiles_kernel(jobs, joining, aliased, slots, *refs):
    if joining:
        parts, refs = refs[:joining], refs[joining:]
    else:
        left, refs = refs[0], refs[1:]
    pieces = []
    for _, _, mine, other, _ in jobs:
        pieces.append((refs[:mine], refs[mine : mine + other]))
        refs = refs[mine + other :]
    if aliased:
        refs = refs[1:]
    out, refs = refs[0], refs[1:]
    if joining:
        left, refs = refs[0], refs[1:]
    rights, (out_buf, out_sem) = refs[:-2], refs[-2:]
    seq, core = lax.axis_index("seq"), lax.rem(lax.axis_index("blk"), 2)
    x, z = lax.rem(seq, 2), seq // 2
    tall = out_buf.shape[1]
    stripe = out.shape[1]
    per = stripe // tall
    if joining:
        for j in range(joining):
            left[j * stripe : (j + 1) * stripe, :] = parts[j][...]

    def store(job, tile, shift, step):
        which = step // per
        round_ = jnp.where(
            which == 0, 0, jnp.where(which == 1, 3 - 2 * core, jnp.where(which == 2, 2, 1 + 2 * core))
        )
        width = rights[job].shape[0]
        slot = lax.rem(step + shift, slots)
        row = pl.multiple_of(lax.rem(step, per) * tall, 16)
        return pltpu.make_async_copy(
            out_buf.at[slot, :, pl.ds(0, width)],
            out.at[round_, pl.ds(row, tall), pl.ds(pl.multiple_of(tile * LANE, LANE), width)],
            out_sem.at[slot],
        )

    before, shift = None, 0
    for job, (form, flipped, _, _, (low, high)) in enumerate(jobs):
        low, high = low * per, high * per
        shift -= low
        right = rights[job]
        tile = (z ^ flipped) * (2 * stripe // LANE) + fill_right(form, right, *pieces[job], x)
        here = functools.partial(store, job, tile, shift % slots)

        def body(step, _, here=here, before=before, right=right, low=low, shift=shift % slots):
            if before is not None:

                @pl.when(step < low + slots)
                def _():
                    before(step - low).wait()

            @pl.when(step >= low + slots)
            def _():
                here(step).wait()

            out_buf[lax.rem(step + shift, slots), :, : right.shape[0]] = lax.dot_general(
                left[pl.ds(pl.multiple_of(step * tall, 16), tall), :],
                right[...],
                (((1,), (1,)), ((), ())),
                preferred_element_type=jnp.float32,
            )
            here(step).start()
            return 0

        lax.fori_loop(low, high, body, 0)
        shift += high
        before = functools.partial(store, job, tile, shift % slots)
    for step in range(slots):
        before(jnp.int32(step)).wait()


def tiles(out, out_shape, left, jobs, slots=3):
    joining = len(left) if isinstance(left, list) else 0
    stripe = out_shape[1]
    depth = (left[0] if joining else left).shape[1]
    tall = stripe // 2
    widths = [width_of(form, stripe) for form, *_ in jobs]
    vmem = pl.BlockSpec(memory_space=pltpu.VMEM)
    anywhere = pl.BlockSpec(memory_space=pl.ANY)
    operands = list(left) if joining else [left]
    for _, _, mine, other, _ in jobs:
        operands += [*mine, *other]
    specs = [vmem] * len(operands)
    aliases = {}
    if out is not None:
        aliases = {len(operands): 0}
        operands.append(out)
        specs.append(anywhere)
    shapes, out_specs = [jax.ShapeDtypeStruct(out_shape, jnp.float32)], [anywhere]
    if joining:
        shapes.append(jax.ShapeDtypeStruct((joining * stripe, depth), jnp.bfloat16))
        out_specs.append(vmem)
    forms = [(form, pair, len(mine), len(other), part) for form, pair, mine, other, part in jobs]
    scratch = sum(widths) * depth * 2 + slots * tall * max(widths) * 4
    columns = sum(width * (part[1] - part[0]) for width, (*_, part) in zip(widths, jobs))
    result = pl.pallas_call(
        functools.partial(tiles_kernel, forms, joining, out is not None, slots),
        out_shape=shapes,
        in_specs=specs,
        out_specs=out_specs,
        scratch_shapes=[pltpu.VMEM((width, depth), jnp.bfloat16) for width in widths]
        + [
            pltpu.VMEM((slots, tall, max(widths)), jnp.float32),
            pltpu.SemaphoreType.DMA((slots,)),
        ],
        input_output_aliases=aliases,
        compiler_params=pltpu.CompilerParams(vmem_limit_bytes=scratch + SPARE_VMEM),
        cost_estimate=pl.CostEstimate(
            flops=2 * stripe * columns * depth,
            bytes_accessed=4 * stripe * columns,
            transcendentals=0,
        ),
        name="tiles",
    )(*operands)
    return result if joining else result[0]


def flip(value, axis, bits):
    count = lax.axis_size(axis)
    return lax.ppermute(value, axis, [(source, source ^ bits) for source in range(count)])


def wait_all(*values):
    return lax.optimization_barrier(values)


def fast_body(scores, counts):
    blocks, parts = lax.axis_size("blk"), lax.axis_size("seq")
    stripe = scores.shape[1] // parts
    out_shape = (blocks, stripe, scores.shape[1])
    pieces = payload(scores, counts, parts)
    order = (6, 7, 4, 5, 2, 3, 1, 0)
    own = center(
        order,
        [flip(pieces[bits], "seq", bits) if bits else pieces[0] for bits in order],
        stripe,
    )

    z = lax.axis_index("seq") // 2
    middle = (z == 1) | (z == 2)
    z1 = flip(own, "seq", 2)
    x_own = flip(own, "seq", 1)
    z3_middle = lax.ppermute(own, "seq", [(2, 4), (4, 2), (3, 5), (5, 3)])
    y_own = flip(own, "blk", 2)
    core_own = flip(own, "blk", 1)
    out, _ = tiles(None, out_shape, [own, core_own], [(FIRST, 0, [own], [], (0, 2))])
    x_own, z1, z3_middle, y_own, out = wait_all(x_own, z1, z3_middle, y_own, out)
    half = stripe // 2
    parts_of = (slice(0, half), slice(half, stripe))
    x_z1 = flip(z1, "seq", 1)
    core_y = flip(y_own, "blk", 1)
    outer_pairs = [(0, 6), (6, 0), (1, 7), (7, 1)]
    z3_outer = [lax.ppermute(own[rows], "seq", outer_pairs) for rows in parts_of]
    every = (0, 4)
    out, left = tiles(
        out,
        out_shape,
        [own, core_own, y_own, core_y],
        [(SECOND, 0, [own], [x_own], every), (FIRST, 1, [z1], [], every)],
    )
    out, z3_outer[0] = wait_all(out, z3_outer[0])
    z3 = [jnp.where(middle, z3_middle[parts_of[0]], z3_outer[0])]
    x_z3, z2 = [flip(z3[0], "seq", 1)], [flip(z3[0], "seq", 2)]
    out, x_z1, z3_outer[1] = wait_all(out, x_z1, z3_outer[1])
    z3.append(jnp.where(middle, z3_middle[parts_of[1]], z3_outer[1]))
    x_z3.append(flip(z3[1], "seq", 1))
    z2.append(flip(z3[1], "seq", 2))
    out = tiles(
        out,
        out_shape,
        left,
        [
            (SECOND, 1, [z1], [x_z1], every),
            (FIRST, 3, z3, [], every),
            (FIRST, 0, [own], [], (2, 4)),
        ],
    )
    out, x_z3[0], z2[1] = wait_all(out, x_z3[0], z2[1])
    x_z2 = [flip(x_z3[0], "seq", 2), flip(z2[1], "seq", 1)]
    out = tiles(out, out_shape, left, [(SECOND, 3, z3, x_z3, every), (FIRST, 2, z2, [], every)])
    return tiles(out, out_shape, left, [(SECOND, 2, z2, x_z2, every)])


def solution(mesh):
    def body(scores, counts):
        stripe_width = scores.shape[1] // mesh.shape["seq"]
        fits = (
            mesh.shape["blk"] == 4
            and mesh.shape["seq"] == 8
            and stripe_width % 64 == 0
            and stripe_width % STATES == 0
            and stripe_width % 64 == 0
        )
        return (fast_body if fits else plain_body)(scores, counts)

    return jax.shard_map(
        body,
        mesh=mesh,
        in_specs=(P("seq", "blk"), P("seq")),
        out_specs=P(None, "seq", "blk"),
        check_vma=False,
    )
```
